512 devices in a mesh: ctx: 64 (over z_hi, y, core), kv: 8 (over x, z_lo).
Axes of the slice: x: 4, y: 8, z: 8 (z_hi: 4, z_lo: 2; z = z_hi * 2 + z_lo), core: 2. Of those that a mesh axis runs over, the one named last changes fastest.
Arguments:
- query: bfloat16 [24576, 4096], P('ctx', 'kv'), may hold values from -9 to 9
- keys: bfloat16 [24576, 1024], P('ctx', 'kv'), may hold values from -8.4 to 8.4
- values: bfloat16 [24576, 1024], P('ctx', 'kv'), may hold values from -6 to 6
- vertical: int32 [8, 16], P('kv'), may hold values from 0 to 383, as said below
- slash: int32 [8, 768], P('kv'), may hold values from 0 to 2048, as said below
- out_weight: bfloat16 [4096, 4096], P('kv', 'ctx'), may hold values from -0.5 to 0.5
Outputs:
- projected: bfloat16 [24576, 4096], P(('ctx', 'kv'))
The draws below stay inside these ranges and needn't reach their ends.
Inputs may be any that keep to these rules, and one draw needn't show every extreme that they name: `vertical`: the 16 blocks of one KV head are distinct, and every KV head lists block 0. `slash`: the 768 offsets of one KV head are distinct, and every KV head lists offset 0.
All inputs are finite; a program needn't handle non-finite values.
Results may differ from the reference program's by a relative error of at most 0.017.
Values may be sent and summed in bfloat16 or wider, within the bound.
No kernel may reach another device: no remote copies, remote signals or barrier semaphores. Data moves between devices by JAX's collectives and lax.ppermute only.
A program may use at most 64 MiB of HBM per device.

```python
import math
import jax
import jax.numpy as jnp
from jax import lax

HD = 128
GROUP = 4
D = 4096
BLK = 64
NV = 16
NS = 768
SLASH_MAX = 2048
TOK_DEV = 384
KVH = 8
H = 32
TOKENS = 24576
NB = 384


def draw_query(key, part):
    key = jax.random.fold_in(key, 5)
    return jnp.clip(1.4 * jax.random.normal(key, (TOKENS, H * HD), jnp.float32), -8.4, 8.4).astype(jnp.bfloat16)


def draw_keys(key, part):
    key = jax.random.fold_in(key, 7)
    return jnp.clip(1.4 * jax.random.normal(key, (TOKENS, KVH * HD), jnp.float32), -8.4, 8.4).astype(jnp.bfloat16)


def draw_vertical(key, part):
    key = jax.random.fold_in(key, 11)
    spread = 2 ** 30 // NB
    scores = jax.random.randint(key, (KVH, NB), 0, spread) * NB + jnp.arange(NB, dtype=jnp.int32)[None, :]
    scores = scores.at[:, 0].set(2 ** 30)
    scores = scores.at[0, NB - 1].set(2 ** 30 - 1)
    return lax.top_k(scores, NV)[1].astype(jnp.int32)


def draw_slash(key, part):
    key = jax.random.fold_in(key, 13)
    count = SLASH_MAX + 1
    spread = 2 ** 30 // count
    scores = jax.random.randint(key, (KVH, count), 0, spread) * count + jnp.arange(count, dtype=jnp.int32)[None, :]
    scores = scores.at[:, 0].set(2 ** 30)
    scores = scores.at[0, SLASH_MAX].set(2 ** 30 - 1)
    return lax.top_k(scores, NS)[1].astype(jnp.int32)


def block_scale(own_key, shape, pieces, smallest, top_value):
    loudness = 1.0
    for position, blocks in pieces:
        heights = jax.random.uniform(jax.random.fold_in(jax.random.fold_in(own_key, 6), position), (blocks,), jnp.float32, smallest / len(pieces), top_value / len(pieces))
        loudness = loudness * jnp.repeat(jnp.exp(heights), shape[position] // blocks).reshape((-1,) + (1,) * (len(shape) - 1 - position))
    return loudness


def bell_draw(rng, shape, deviation, bound, pieces=(), kind=jnp.bfloat16):
    values = jax.random.normal(rng, shape, jnp.float32) * deviation
    if len(pieces) > 0:
        values = block_scale(rng, shape, pieces, -0.22, 0.18) * values
    return jnp.clip(values, min=-bound, max=bound).astype(kind)


def setup_inputs(seed: int = 0) -> dict:
    key_list = jax.random.split(jax.random.key(seed), 7)
    return {
        "query": draw_query(jax.random.fold_in(key_list[6], 71), 0),
        "keys": draw_keys(jax.random.fold_in(key_list[6], 71), 0),
        "values": bell_draw(key_list[2], (TOKENS, KVH * HD), 1.0, 6.0, ((0, 64), (1, 8))),
        "vertical": draw_vertical(jax.random.fold_in(key_list[6], 71), 0),
        "slash": draw_slash(jax.random.fold_in(key_list[6], 71), 0),
        "out_weight": bell_draw(key_list[5], (H * HD, D), HD ** -0.5, 0.5, ((0, 8), (1, 64))),
    }


def attend_block(block_id, queries, key_pad, value_pad, far_keys, far_values, listed, offsets):
    start = (block_id * TOK_DEV).astype(jnp.int32)
    q_rows = lax.dynamic_slice_in_dim(queries, start, TOK_DEV, 0).reshape(TOK_DEV, GROUP, HD).astype(jnp.float32)
    positions = start + jnp.arange(TOK_DEV, dtype=jnp.int32)
    scale = 1.0 / math.sqrt(HD)
    far_scores = jnp.einsum('tgd,kd->gtk', q_rows, far_keys.astype(jnp.float32)) * scale
    far_pos = (listed[:, None] * BLK + jnp.arange(BLK, dtype=jnp.int32)[None, :]).reshape(-1)
    far_ok = far_pos[None, :] <= positions[:, None]
    far_scores = jnp.where(far_ok[None], far_scores, -1e+30)
    starts = (SLASH_MAX + start - offsets).astype(jnp.int32)
    line_keys = jax.vmap(lambda s: lax.dynamic_slice_in_dim(key_pad, s, TOK_DEV, 0))(starts)
    line_values = jax.vmap(lambda s: lax.dynamic_slice_in_dim(value_pad, s, TOK_DEV, 0))(starts)
    line_scores = jnp.einsum('tgd,std->gst', q_rows, line_keys.astype(jnp.float32)) * scale
    line_pos = positions[None, :] - offsets[:, None]
    member = jnp.any((line_pos // BLK)[:, :, None] == listed[None, None, :], axis=-1)
    line_ok = (line_pos >= 0) & jnp.logical_not(member)
    line_scores = jnp.where(line_ok[None], line_scores, -1e+30)
    top = jnp.maximum(lax.optimization_barrier(jnp.max(far_scores, axis=-1)), lax.optimization_barrier(jnp.max(line_scores, axis=1)))
    far_weights = jnp.exp(far_scores - top[:, :, None])
    line_weights = jnp.exp(line_scores - top[:, None, :])
    total = lax.optimization_barrier(jnp.sum(far_weights, axis=-1)) + lax.optimization_barrier(jnp.sum(line_weights, axis=1))
    far_rounded = far_weights.astype(jnp.bfloat16).astype(jnp.float32)
    line_rounded = line_weights.astype(jnp.bfloat16).astype(jnp.float32)
    mixed = jnp.einsum('gtk,kd->tgd', far_rounded, far_values.astype(jnp.float32))
    mixed = mixed + jnp.einsum('gst,std->tgd', line_rounded, line_values.astype(jnp.float32))
    return (mixed / total.T[:, :, None]).astype(jnp.bfloat16).reshape(TOK_DEV, GROUP * HD)

def reference(query, keys, values, vertical, slash, out_weight):

    def head_term(carry, head):
        keys_head = lax.dynamic_slice_in_dim(keys, head * HD, HD, 1)
        values_head = lax.dynamic_slice_in_dim(values, head * HD, HD, 1)
        queries = lax.dynamic_slice_in_dim(query, head * GROUP * HD, GROUP * HD, 1)
        listed = lax.dynamic_index_in_dim(vertical, head, 0, keepdims=False)
        offsets = lax.dynamic_index_in_dim(slash, head, 0, keepdims=False)
        far_keys = keys_head.reshape(NB, BLK, HD)[listed].reshape(NV * BLK, HD)
        far_values = values_head.reshape(NB, BLK, HD)[listed].reshape(NV * BLK, HD)
        key_pad = jnp.pad(keys_head, ((SLASH_MAX, 0), (0, 0)))
        value_pad = jnp.pad(values_head, ((SLASH_MAX, 0), (0, 0)))
        blocks = jnp.arange(TOKENS // TOK_DEV, dtype=jnp.int32)
        attended = lax.map(lambda b: attend_block(b, queries, key_pad, value_pad, far_keys, far_values, listed, offsets), blocks)
        attended = attended.reshape(TOKENS, GROUP * HD)
        weight_rows = lax.dynamic_slice_in_dim(out_weight, head * GROUP * HD, GROUP * HD, 0)
        term = jnp.dot(attended, weight_rows, preferred_element_type=jnp.float32).astype(jnp.bfloat16)
        term = lax.optimization_barrier(term)
        return (carry + term.astype(jnp.float32), None)
    start_sum = jnp.zeros((TOKENS, D), jnp.float32)
    summed, _ = lax.scan(head_term, start_sum, jnp.arange(KVH, dtype=jnp.int32))
    return summed.astype(jnp.bfloat16)
```

```python
import functools
import math

import jax
import jax.numpy as jnp
from jax import lax
from jax.experimental import pallas as pl
from jax.experimental.pallas import tpu as pltpu
from jax.sharding import Mesh, PartitionSpec as P

BLK = 64
SLASH_MAX = 2048
HD = 128
GROUP = 4
QB = 128
MASKED = -1e30
CTX = ("zh", "y", "c")
KV = ("x", "zl")
SCALE = math.log2(math.e) / math.sqrt(HD)
NT = (((1,), (1,)), ((), ()))
VMEM_LIMIT = 48 * 1024 * 1024


def vmem(n):
    return [pl.BlockSpec(memory_space=pltpu.VMEM)] * n


def pick_kernel(ids_ref, k_ref, v_ref, pair_ref, keep_ref, send_ref):
    rows = k_ref.shape[0]
    pair_ref[0] = k_ref[...]
    pair_ref[1] = v_ref[...]
    half = keep_ref.shape[0]
    for slot in range(2 * half):
        block = ids_ref[slot]
        here = jnp.logical_and(block >= 0, block < rows // BLK)
        row = pl.multiple_of(jnp.clip(block, 0, rows // BLK - 1) * BLK, BLK)
        out = keep_ref if slot < half else send_ref
        for part, ref in enumerate((k_ref, v_ref)):
            got = ref[pl.ds(row, BLK), :].astype(jnp.float32)
            out[slot % half, part] = jnp.where(here, got, 0.0).astype(jnp.bfloat16)


def stacked_queries(q_ref, first):
    return jnp.concatenate(
        [q_ref[pl.ds(first, QB), h * HD : (h + 1) * HD] for h in range(GROUP)], axis=0
    )


def lane_fold(op, x):
    out = x[:, :HD]
    for i in range(1, x.shape[1] // HD):
        out = op(out, x[:, i * HD : (i + 1) * HD])
    return out


def band_kernel(q_ref, line_ref, col_ref, *refs):
    pieces, (acc_ref, top_ref, sum_ref), (diag, bias, kwin, vwin, s_scr) = refs[:7], refs[7:10], refs[10:]
    rows = q_ref.shape[0]
    span = SLASH_MAX + QB
    lead = 7 * rows - rows - SLASH_MAX
    for i, piece in enumerate(pieces):
        kwin[i * rows : (i + 1) * rows] = piece[0]
        vwin[i * rows : (i + 1) * rows] = piece[1]
    diag[...] = pltpu.roll(
        jnp.broadcast_to(line_ref[...], (QB, span)), 0, 1, stride=1, stride_axis=0
    )
    chunks = [(at, min(256, span - at)) for at in range(0, span, 256)]

    @pl.loop(0, rows // QB)
    def _(step):
        first = pl.multiple_of(step * QB, QB)
        base = pl.multiple_of(lead + step * QB, QB)
        bias[...] = diag[...] + col_ref[:, pl.ds(base, span)]
        q = stacked_queries(q_ref, first)
        top = jnp.full((GROUP * QB, HD), MASKED, jnp.float32)
        for at, width in chunks:
            k = kwin[pl.ds(base + at, width), :]
            s = lax.dot_general(q, k, NT, preferred_element_type=jnp.float32)
            b = bias[:, at : at + width]
            s = s + jnp.concatenate([b] * GROUP, axis=0)
            s_scr[:, at : at + width] = s
            top = jnp.maximum(top, lane_fold(jnp.maximum, s))
        top = jnp.max(top, axis=1, keepdims=True)
        shift = top * SCALE
        acc = jnp.zeros((GROUP * QB, HD), jnp.float32)
        total = jnp.zeros((GROUP * QB, HD), jnp.float32)
        for at, width in chunks:
            p = jnp.exp2(s_scr[:, at : at + width] * SCALE - shift)
            total = total + lane_fold(jnp.add, p)
            v = vwin[pl.ds(base + at, width), :]
            acc = acc + jnp.dot(p.astype(jnp.bfloat16), v, preferred_element_type=jnp.float32)
        acc_ref[step] = acc
        sum_ref[step] = total
        top_ref[step] = jnp.broadcast_to(top, (GROUP * QB, HD))


def far_kernel(place_ref, q_ref, pos_ref, mine_ref, other_ref, acc_ref, top_ref, sum_ref,
               w_mine, w_other, out_ref, w_scr, kfar, vfar, attended, sems):
    rows = q_ref.shape[0]
    core = place_ref[1]
    n_y, n_zh = w_mine.shape[0], w_mine.shape[1]
    copies = []
    for i, (src, at) in enumerate(((w_mine, core), (w_other, 1 - core))):
        for z in range(n_zh):
            copy = pltpu.make_async_copy(
                src.at[:, z], w_scr.at[pl.ds(z * n_y, n_y), at], sems.at[i * n_zh + z]
            )
            copy.start()
            copies.append(copy)
    half = mine_ref.shape[0]
    for i in range(half):
        for j, ref in enumerate((mine_ref, other_ref)):
            at = (j * half + i) * BLK
            kfar[at : at + BLK] = ref[i, 0]
            vfar[at : at + BLK] = ref[i, 1]
    n_far = kfar.shape[0]
    chunks = [(at, 256) for at in range(0, n_far, 256)]

    @pl.loop(0, rows // QB)
    def _(step):
        first = pl.multiple_of(step * QB, QB)
        q = stacked_queries(q_ref, first)
        q_pos = place_ref[0] * rows + first + lax.broadcasted_iota(jnp.int32, (QB, 256), 0)
        band_top = top_ref[step]
        top = band_top
        scores = []
        for at, width in chunks:
            s = lax.dot_general(q, kfar[at : at + width], NT, preferred_element_type=jnp.float32)
            ok = pos_ref[:, at : at + width] <= q_pos
            b = jnp.where(ok, 0.0, MASKED)
            s = s + jnp.concatenate([b] * GROUP, axis=0)
            scores.append(s)
            top = jnp.maximum(top, lane_fold(jnp.maximum, s))
        top = jnp.max(top, axis=1, keepdims=True)
        shift = top * SCALE
        fade = jnp.exp2(band_top * SCALE - shift)
        acc = acc_ref[step] * fade
        total = sum_ref[step] * fade
        for (at, width), s in zip(chunks, scores):
            p = jnp.exp2(s * SCALE - shift)
            total = total + lane_fold(jnp.add, p)
            acc = acc + jnp.dot(
                p.astype(jnp.bfloat16), vfar[at : at + width], preferred_element_type=jnp.float32
            )
        out = (acc / jnp.sum(total, axis=1, keepdims=True)).astype(jnp.bfloat16)
        for h in range(GROUP):
            attended[pl.ds(first, QB), h * HD : (h + 1) * HD] = out[h * QB : (h + 1) * QB]

    for copy in copies:
        copy.wait()
    width = 512
    per = width // w_scr.shape[2] // 2

    @pl.loop(0, out_ref.shape[1] // width)
    def _(n):
        w = w_scr[pl.ds(n * per, per)].reshape(width, GROUP * HD)
        at = pl.multiple_of(n * width, width)
        out_ref[:, pl.ds(at, width)] = lax.dot_general(
            attended[...], w, NT, preferred_element_type=jnp.float32
        ).astype(jnp.bfloat16)


def swap(x):
    return lax.ppermute(x, "c", [(0, 1), (1, 0)])


def spread(x, axis):
    n = lax.axis_size(axis)
    return lax.all_to_all(jnp.broadcast_to(x[None], (n,) + x.shape), axis, 0, 0, tiled=True)


def summed(x):
    return jnp.sum(x.astype(jnp.float32), axis=0).astype(jnp.bfloat16)


def body(query, keys, values, vertical, slash, out_weight):
    rows, width = keys.shape
    n_ctx = lax.axis_size(CTX)
    place = lax.axis_index(CTX)
    core = lax.axis_index("c")
    listed = vertical[0]
    offsets = slash[0]
    n_listed = listed.shape[0]
    half = n_listed // 2
    per_shard = rows // BLK
    span = SLASH_MAX + QB
    bf16, f32 = jnp.bfloat16, jnp.float32

    ordered = jnp.where(core == 0, listed, jnp.roll(listed, half))
    pair, keep, send = pl.pallas_call(
        pick_kernel,
        in_specs=[pl.BlockSpec(memory_space=pltpu.SMEM)] + vmem(2),
        out_specs=vmem(3),
        out_shape=[
            jax.ShapeDtypeStruct((2, rows, width), bf16),
            jax.ShapeDtypeStruct((half, 2, BLK, width), bf16),
            jax.ShapeDtypeStruct((half, 2, BLK, width), bf16),
        ],
        name="pick",
    )(ordered - place * per_shard, keys, values)

    blocks = keep + swap(send)
    blocks = summed(lax.all_to_all(blocks, "y", 0, 0, tiled=True))
    blocks = summed(spread(blocks, "zh"))
    far_mine = spread(blocks, "y")
    far_other = swap(far_mine)

    ahead = [(i, i + 2) for i in range(n_ctx - 2)]
    own = [pair]
    for _ in range(3):
        own.append(lax.ppermute(own[-1], CTX, ahead))
    other = [swap(jnp.where(core == 0, own[k - 1], own[k])) for k in (1, 2, 3)]
    band = [own[3], other[2], own[2], other[1], own[1], other[0], own[0]]

    w = spread(out_weight.T, "zh")
    w_mine = lax.all_gather(w, "y", axis=0, tiled=False)
    w_other = swap(w_mine)

    distance = SLASH_MAX - jnp.arange(span, dtype=jnp.int32)
    line = jnp.where(jnp.any(distance[None, :] == offsets[:, None], axis=0), 0.0, MASKED)
    k_pos = (place - 6) * rows + jnp.arange(7 * rows, dtype=jnp.int32)
    is_listed = jnp.any((k_pos // BLK)[None, :] == listed[:, None], axis=0)
    column = jnp.where((k_pos >= 0) & jnp.logical_not(is_listed), 0.0, MASKED)
    far_pos = ordered[:, None] * BLK + jnp.arange(BLK, dtype=jnp.int32)[None, :]

    steps = rows // QB
    stats = jax.ShapeDtypeStruct((steps, GROUP * QB, HD), f32)
    acc, top, total = pl.pallas_call(
        band_kernel,
        in_specs=vmem(10),
        out_specs=vmem(3),
        out_shape=[stats, stats, stats],
        scratch_shapes=[
            pltpu.VMEM((QB, span), f32),
            pltpu.VMEM((QB, span), f32),
            pltpu.VMEM((7 * rows, HD), bf16),
            pltpu.VMEM((7 * rows, HD), bf16),
            pltpu.VMEM((GROUP * QB, span), f32),
        ],
        compiler_params=pltpu.CompilerParams(vmem_limit_bytes=VMEM_LIMIT),
        cost_estimate=pl.CostEstimate(
            flops=4 * rows * GROUP * HD * span,
            bytes_accessed=8_000_000,
            transcendentals=rows * GROUP * span,
        ),
        name="band",
    )(query, line[None], column[None], *band)

    n_far = n_listed * BLK
    d_model = out_weight.shape[1] * n_ctx
    partial_sum = pl.pallas_call(
        far_kernel,
        in_specs=[pl.BlockSpec(memory_space=pltpu.SMEM)] + vmem(7)
        + [pl.BlockSpec(memory_space=pl.ANY)] * 2,
        out_specs=pl.BlockSpec(memory_space=pltpu.VMEM),
        out_shape=jax.ShapeDtypeStruct((rows, d_model), bf16),
        scratch_shapes=[
            pltpu.VMEM((n_ctx // 2, 2, out_weight.shape[1], GROUP * HD), bf16),
            pltpu.VMEM((n_far, HD), bf16),
            pltpu.VMEM((n_far, HD), bf16),
            pltpu.VMEM((rows, GROUP * HD), bf16),
            pltpu.SemaphoreType.DMA((2 * lax.axis_size("zh"),)),
        ],
        compiler_params=pltpu.CompilerParams(vmem_limit_bytes=VMEM_LIMIT),
        cost_estimate=pl.CostEstimate(
            flops=4 * rows * GROUP * HD * n_far + 2 * rows * GROUP * HD * d_model,
            bytes_accessed=10_000_000,
            transcendentals=rows * GROUP * n_far,
        ),
        name="far",
    )(
        jnp.stack([place, core]).astype(jnp.int32),
        query,
        far_pos.reshape(1, n_far),
        far_mine,
        far_other,
        acc,
        top,
        total,
        w_mine,
        w_other,
    )
    received = lax.all_to_all(partial_sum.reshape(8, rows // 8, d_model), KV, 0, 0, tiled=True)
    return summed(received)


def solution(mesh):
    fine = Mesh(mesh.devices.reshape(4, 8, 2, 4, 2), CTX + KV)
    return jax.shard_map(
        body,
        mesh=fine,
        in_specs=(
            P(CTX, KV),
            P(CTX, KV),
            P(CTX, KV),
            P(KV, None),
            P(KV, None),
            P(KV, CTX),
        ),
        out_specs=P(CTX + KV, None),
        check_vma=False,
    )
```

```python
import functools
import math

import jax
import jax.numpy as jnp
from jax import lax
from jax.experimental import pallas as pl
from jax.experimental.pallas import tpu as pltpu
from jax.sharding import Mesh, PartitionSpec as P

BLK = 64
SLASH_MAX = 2048
HD = 128
GROUP = 4
QB = 128
MASKED = -1e30
CTX = ("zh", "y", "c")
KV = ("x", "zl")
ZY = ("zh", "y")
SCALE = math.log2(math.e) / math.sqrt(HD)
NT = (((1,), (1,)), ((), ()))
VMEM_LIMIT = 48 * 1024 * 1024


def vmem(n):
    return [pl.BlockSpec(memory_space=pltpu.VMEM)] * n


def pick_kernel(place_ref, listed_ref, k_ref, v_ref, pair_ref, keep_ref, send_ref):
    rows = k_ref.shape[0]
    base = place_ref[0] * (rows // BLK)
    flip = place_ref[1] * keep_ref.shape[0]
    pair_ref[0] = k_ref[...]
    pair_ref[1] = v_ref[...]
    half = keep_ref.shape[0]
    for slot in range(2 * half):
        block = listed_ref[0, (slot + flip) % (2 * half)] - base
        here = jnp.logical_and(block >= 0, block < rows // BLK)
        row = pl.multiple_of(jnp.clip(block, 0, rows // BLK - 1) * BLK, BLK)
        out = keep_ref if slot < half else send_ref
        for part, ref in enumerate((k_ref, v_ref)):
            got = ref[pl.ds(row, BLK), :].astype(jnp.float32)
            out[slot % half, part] = jnp.where(here, got, 0.0).astype(jnp.bfloat16)


def choose_kernel(place_ref, *refs):
    own, out_ref = refs[:4], refs[4]
    for core in (0, 1):
        @pl.when(place_ref[1] == core)
        def _(core=core):
            for k in range(3):
                out_ref[k] = own[k + core][...]


def total_kernel(x_ref, *refs):
    out_ref = refs[-1]
    total = jnp.sum(x_ref[...].astype(jnp.float32), axis=0).astype(jnp.bfloat16)
    for i in range(out_ref.shape[0]):
        out_ref[i] = total


def stacked_queries(q_ref, first):
    return jnp.concatenate(
        [q_ref[pl.ds(first, QB), h * HD : (h + 1) * HD] for h in range(GROUP)], axis=0
    )


def lane_fold(op, x):
    out = x[:, :HD]
    for i in range(1, x.shape[1] // HD):
        out = op(out, x[:, i * HD : (i + 1) * HD])
    return out


def collect_kernel(place_ref, own, up, down, far_lo, far_hi, late, later, out_ref, sems):
    n_zh, n_y = out_ref.shape[:2]
    me = place_ref[0] // (2 * n_y)
    mid = n_y // 2
    far = out_ref.at[lax.rem(me + 2, n_zh)]
    pieces = (
        (own, out_ref.at[me]),
        (up, out_ref.at[lax.rem(me + n_zh - 1, n_zh)]),
        (down, out_ref.at[lax.rem(me + 1, n_zh)]),
        (far_lo, far.at[:mid]),
        (far_hi, far.at[mid:]),
    )
    copies = [pltpu.make_async_copy(a, b, sems.at[i]) for i, (a, b) in enumerate(pieces)]
    for copy in copies:
        copy.start()
    for copy in copies:
        copy.wait()


def band_kernel(place_ref, listed_ref, q_ref, slash_ref, *refs):
    own, other = refs[:4], refs[4]
    (acc_ref, top_ref, sum_ref), (diag, col, bias, kwin, vwin, s_scr) = refs[5:8], refs[8:]
    rows = q_ref.shape[0]
    span = SLASH_MAX + QB
    lead = 7 * rows - rows - SLASH_MAX
    for i in range(7):
        piece = own[3 - i // 2] if i % 2 == 0 else other.at[2 - i // 2]
        kwin[i * rows : (i + 1) * rows] = piece[0]
        vwin[i * rows : (i + 1) * rows] = piece[1]

    at = SLASH_MAX - slash_ref[...]
    n_off = at.shape[1]
    major = lax.broadcasted_iota(jnp.int32, (32, n_off), 0) == at // HD
    minor = lax.broadcasted_iota(jnp.int32, (HD, n_off), 0) == at % HD
    hits = lax.dot_general(
        jnp.where(major, 1.0, 0.0).astype(jnp.bfloat16),
        jnp.where(minor, 1.0, 0.0).astype(jnp.bfloat16),
        NT,
        preferred_element_type=jnp.float32,
    )
    line = jnp.where(hits > 0.5, 0.0, MASKED)
    for i in range(span // HD):
        bias[:, i * HD : (i + 1) * HD] = jnp.broadcast_to(line[i : i + 1], (QB, HD))
    diag[...] = pltpu.roll(bias[...], 0, 1, stride=1, stride_axis=0)

    block = lax.broadcasted_iota(jnp.int32, (1, 7 * rows), 1) // BLK
    block = block + (place_ref[0] - 6) * (rows // BLK)
    out = block < 0
    for i in range(listed_ref.shape[1]):
        out = jnp.logical_or(out, block == listed_ref[0, i])
    col[...] = jnp.where(out, MASKED, 0.0)

    chunks = [(at, min(256, span - at)) for at in range(0, span, 256)]

    @pl.loop(0, rows // QB)
    def _(step):
        first = pl.multiple_of(step * QB, QB)
        base = pl.multiple_of(lead + step * QB, QB)
        bias[...] = diag[...] + col[:, pl.ds(base, span)]
        q = stacked_queries(q_ref, first)
        top = jnp.full((GROUP * QB, HD), MASKED, jnp.float32)
        for at, width in chunks:
            k = kwin[pl.ds(base + at, width), :]
            s = lax.dot_general(q, k, NT, preferred_element_type=jnp.float32)
            b = bias[:, at : at + width]
            s = s + jnp.concatenate([b] * GROUP, axis=0)
            s_scr[:, at : at + width] = s
            top = jnp.maximum(top, lane_fold(jnp.maximum, s))
        top = jnp.max(top, axis=1, keepdims=True)
        shift = top * SCALE
        acc = jnp.zeros((GROUP * QB, HD), jnp.float32)
        total = jnp.zeros((GROUP * QB, HD), jnp.float32)
        for at, width in chunks:
            p = jnp.exp2(s_scr[:, at : at + width] * SCALE - shift)
            total = total + lane_fold(jnp.add, p)
            v = vwin[pl.ds(base + at, width), :]
            acc = acc + jnp.dot(p.astype(jnp.bfloat16), v, preferred_element_type=jnp.float32)
        acc_ref[step] = acc
        sum_ref[step] = total
        top_ref[step] = jnp.broadcast_to(top, (GROUP * QB, HD))


def far_kernel(place_ref, listed_ref, q_ref, mine_ref, other_ref, acc_ref, top_ref, sum_ref,
               attended, kfar, vfar):
    rows = q_ref.shape[0]
    half = mine_ref.shape[0]
    flip = place_ref[1] * half
    for i in range(half):
        for j, ref in enumerate((mine_ref, other_ref)):
            at = (j * half + i) * BLK
            kfar[at : at + BLK] = ref[i, 0]
            vfar[at : at + BLK] = ref[i, 1]
    n_far = kfar.shape[0]
    chunks = [(at, 256) for at in range(0, n_far, 256)]
    lane = lax.broadcasted_iota(jnp.int32, (1, 256), 1)
    positions = []
    for at, width in chunks:
        pos = jnp.zeros((1, 256), jnp.int32)
        for i in range(width // BLK):
            slot = (at // BLK + i + flip) % (2 * half)
            pos = jnp.where(lane // BLK == i, listed_ref[0, slot], pos)
        positions.append(pos * BLK + lane % BLK)

    @pl.loop(0, rows // QB)
    def _(step):
        first = pl.multiple_of(step * QB, QB)
        q = stacked_queries(q_ref, first)
        q_pos = place_ref[0] * rows + first + lax.broadcasted_iota(jnp.int32, (QB, 256), 0)
        band_top = top_ref[step]
        top = band_top
        scores = []
        for (at, width), pos in zip(chunks, positions):
            s = lax.dot_general(q, kfar[at : at + width], NT, preferred_element_type=jnp.float32)
            b = jnp.where(pos <= q_pos, 0.0, MASKED)
            s = s + jnp.concatenate([b] * GROUP, axis=0)
            scores.append(s)
            top = jnp.maximum(top, lane_fold(jnp.maximum, s))
        top = jnp.max(top, axis=1, keepdims=True)
        shift = top * SCALE
        fade = jnp.exp2(band_top * SCALE - shift)
        acc = acc_ref[step] * fade
        total = sum_ref[step] * fade
        for (at, width), s in zip(chunks, scores):
            p = jnp.exp2(s * SCALE - shift)
            total = total + lane_fold(jnp.add, p)
            acc = acc + jnp.dot(
                p.astype(jnp.bfloat16), vfar[at : at + width], preferred_element_type=jnp.float32
            )
        out = (acc / jnp.sum(total, axis=1, keepdims=True)).astype(jnp.bfloat16)
        for h in range(GROUP):
            attended[pl.ds(first, QB), h * HD : (h + 1) * HD] = out[h * QB : (h + 1) * QB]


def project_kernel(place_ref, att_ref, w_mine, w_other, out_ref, w_scr, sem_in, out_scr, sem_out):
    core = place_ref[1]
    n_zh, n_y = w_mine.shape[0], w_mine.shape[1]
    width = 512
    per = width // w_scr.shape[2] // 2
    span = out_ref.shape[1] // n_zh

    def fetch(z, i):
        src, at = ((w_mine, core), (w_other, 1 - core))[i]
        dst = w_scr.at[pl.ds(z * n_y, n_y), at]
        return pltpu.make_async_copy(src.at[z], dst, sem_in.at[z, i])

    def store(z):
        return pltpu.make_async_copy(
            out_scr.at[z], out_ref.at[:, z * span : (z + 1) * span], sem_out.at[z]
        )

    for z in range(n_zh):
        fetch(z, 0).start()
        fetch(z, 1).start()
    for z in range(n_zh):
        fetch(z, 0).wait()
        fetch(z, 1).wait()
        for n in range(span // width):
            w = w_scr[z * n_y + n * per : z * n_y + (n + 1) * per].reshape(width, GROUP * HD)
            out_scr[z, :, n * width : (n + 1) * width] = lax.dot_general(
                att_ref[...], w, NT, preferred_element_type=jnp.float32
            ).astype(jnp.bfloat16)
        store(z).start()
    for z in range(n_zh):
        store(z).wait()


def after(x, *others):
    return pl.pallas_call(
        lambda *refs: None,
        in_specs=[pl.BlockSpec(memory_space=pl.ANY)] * (1 + len(others)),
        out_specs=pl.BlockSpec(memory_space=pl.ANY),
        out_shape=jax.ShapeDtypeStruct(x.shape, x.dtype),
        input_output_aliases={0: 0},
        name="after",
    )(x, *others)


def swap(x):
    return lax.ppermute(x, "c", [(0, 1), (1, 0)])


def spread(x, axis):
    n = lax.axis_size(axis)
    return lax.all_to_all(jnp.broadcast_to(x[None], (n,) + x.shape), axis, 0, 0, tiled=True)


def summed(x):
    return jnp.sum(x.astype(jnp.float32), axis=0).astype(jnp.bfloat16)


def body(query, keys, values, vertical, slash, out_weight):
    rows, width = keys.shape
    n_ctx = lax.axis_size(CTX)
    n_y, n_zh = lax.axis_size("y"), lax.axis_size("zh")
    place = lax.axis_index(CTX)
    core = lax.axis_index("c")
    half = vertical.shape[1] // 2
    cols, inner = out_weight.shape[1], out_weight.shape[0]
    span = SLASH_MAX + QB
    bf16, f32 = jnp.bfloat16, jnp.float32
    smem = [pl.BlockSpec(memory_space=pltpu.SMEM)]
    hbm = [pl.BlockSpec(memory_space=pl.ANY)]
    where = jnp.stack([place, core]).astype(jnp.int32)

    def shape(*dims, dtype=bf16):
        return jax.ShapeDtypeStruct(dims, dtype)

    pair, keep, send = pl.pallas_call(
        pick_kernel,
        in_specs=smem * 2 + vmem(2),
        out_specs=vmem(3),
        out_shape=[
            shape(2, rows, width),
            shape(half, 2, BLK, width),
            shape(half, 2, BLK, width),
        ],
        name="pick",
    )(where, vertical, keys, values)

    up = [(i, (i + 1) % n_zh) for i in range(n_zh)]
    down = [(i, (i - 1) % n_zh) for i in range(n_zh)]
    w = spread(out_weight.T, "y")
    w_up = lax.ppermute(w, "zh", up)
    w_down = lax.ppermute(w, "zh", down)

    own = [pair]
    for k in (1, 2, 3):
        own.append(lax.ppermute(pair, CTX, [(i, i + 2 * k) for i in range(n_ctx - 2 * k)]))

    blocks = (keep + swap(send)).reshape(n_zh * n_y, -1, width)
    parts = lax.all_to_all(after(blocks, w), ZY, 0, 0, tiled=True)
    parts = pl.pallas_call(
        total_kernel, in_specs=vmem(1) + hbm * 5, out_specs=vmem(1)[0],
        out_shape=shape(*parts.shape), name="total",
    )(parts, w_up, w_down, *own[1:])
    far_mine = lax.all_to_all(parts, ZY, 0, 0, tiled=True).reshape(half, 2, BLK, width)
    far_other = swap(far_mine)

    other = swap(pl.pallas_call(
        choose_kernel, in_specs=smem + vmem(4), out_specs=vmem(1)[0],
        out_shape=shape(3, 2, rows, width), name="choose",
    )(where, *own))

    steps = rows // QB
    stats = shape(steps, GROUP * QB, HD, dtype=f32)
    acc, top, total = pl.pallas_call(
        band_kernel,
        in_specs=smem * 2 + vmem(7),
        out_specs=vmem(3),
        out_shape=[stats, stats, stats],
        scratch_shapes=[
            pltpu.VMEM((QB, span), f32),
            pltpu.VMEM((1, 7 * rows), f32),
            pltpu.VMEM((QB, span), f32),
            pltpu.VMEM((7 * rows, HD), bf16),
            pltpu.VMEM((7 * rows, HD), bf16),
            pltpu.VMEM((GROUP * QB, span), f32),
        ],
        compiler_params=pltpu.CompilerParams(vmem_limit_bytes=VMEM_LIMIT),
        cost_estimate=pl.CostEstimate(
            flops=8 * rows * GROUP * HD * span,
            bytes_accessed=8_000_000,
            transcendentals=rows * GROUP * span,
        ),
        name="band",
    )(where, vertical, query, slash, *own, other)

    mid = n_y // 2
    w_mine = pl.pallas_call(
        collect_kernel,
        in_specs=smem + hbm * 7,
        out_specs=hbm[0],
        out_shape=shape(n_zh, *w.shape),
        scratch_shapes=[pltpu.SemaphoreType.DMA((5,))],
        name="collect",
    )(
        where, w, w_up, w_down,
        lax.ppermute(w_up[:mid], "zh", up),
        lax.ppermute(w_down[mid:], "zh", down),
        far_mine, acc,
    )
    w_other = swap(w_mine)

    n_far = 2 * half * BLK
    attended = pl.pallas_call(
        far_kernel,
        in_specs=smem * 2 + vmem(6),
        out_specs=vmem(1)[0],
        out_shape=shape(rows, GROUP * HD),
        scratch_shapes=[pltpu.VMEM((n_far, HD), bf16), pltpu.VMEM((n_far, HD), bf16)],
        compiler_params=pltpu.CompilerParams(vmem_limit_bytes=VMEM_LIMIT),
        cost_estimate=pl.CostEstimate(
            flops=8 * rows * GROUP * HD * n_far,
            bytes_accessed=8_000_000,
            transcendentals=rows * GROUP * n_far,
        ),
        name="far",
    )(where, vertical, query, far_mine, far_other, acc, top, total)

    d_model = cols * n_ctx
    partial_sum = pl.pallas_call(
        project_kernel,
        in_specs=smem + vmem(1) + hbm * 2,
        out_specs=hbm[0],
        out_shape=shape(rows, d_model),
        scratch_shapes=[
            pltpu.VMEM((n_zh * n_y, 2, cols, inner), bf16),
            pltpu.SemaphoreType.DMA((n_zh, 2)),
            pltpu.VMEM((n_zh, rows, d_model // n_zh), bf16),
            pltpu.SemaphoreType.DMA((n_zh,)),
        ],
        compiler_params=pltpu.CompilerParams(vmem_limit_bytes=VMEM_LIMIT),
        cost_estimate=pl.CostEstimate(
            flops=2 * rows * inner * d_model, bytes_accessed=8_000_000, transcendentals=0
        ),
        name="project",
    )(where, attended, w_mine, w_other)
    received = lax.all_to_all(partial_sum.reshape(8, rows // 8, d_model), KV, 0, 0, tiled=True)
    return summed(received)


def solution(mesh):
    fine = Mesh(mesh.devices.reshape(4, 8, 2, 4, 2), CTX + KV)
    return jax.shard_map(
        body,
        mesh=fine,
        in_specs=(
            P(CTX, KV),
            P(CTX, KV),
            P(CTX, KV),
            P(KV, None),
            P(KV, None),
            P(KV, CTX),
        ),
        out_specs=P(CTX + KV, None),
        check_vma=False,
    )
```

```python
import functools
import math

import jax
import jax.numpy as jnp
from jax import lax
from jax.experimental import pallas as pl
from jax.experimental.pallas import tpu as pltpu
from jax.sharding import Mesh, PartitionSpec as P

BLK = 64
SLASH_MAX = 2048
HD = 128
GROUP = 4
QB = 128
MASKED = -1e30
CTX = ("zh", "y", "c")
KV = ("x", "zl")
ZY = ("zh", "y")
SCALE = math.log2(math.e) / math.sqrt(HD)
NT = (((1,), (1,)), ((), ()))
VMEM_LIMIT = 48 * 1024 * 1024


def vmem(n):
    return [pl.BlockSpec(memory_space=pltpu.VMEM)] * n


def pick_kernel(place_ref, listed_ref, k_ref, v_ref, keep_ref, send_ref):
    rows = k_ref.shape[0]
    base = place_ref[0] * (rows // BLK)
    flip = place_ref[1] * keep_ref.shape[0]
    half = keep_ref.shape[0]
    for slot in range(2 * half):
        block = listed_ref[0, (slot + flip) % (2 * half)] - base
        here = jnp.logical_and(block >= 0, block < rows // BLK)
        row = pl.multiple_of(jnp.clip(block, 0, rows // BLK - 1) * BLK, BLK)
        out = keep_ref if slot < half else send_ref
        for part, ref in enumerate((k_ref, v_ref)):
            got = ref[pl.ds(row, BLK), :].astype(jnp.float32)
            out[slot % half, part] = jnp.where(here, got, 0.0).astype(jnp.bfloat16)


def merge_kernel(keep_ref, got_ref, k_ref, v_ref, blocks_ref, pair_ref):
    total = keep_ref[...].astype(jnp.float32) + got_ref[...].astype(jnp.float32)
    blocks_ref[...] = total.astype(jnp.bfloat16)
    pair_ref[0] = k_ref[...]
    pair_ref[1] = v_ref[...]


def choose_kernel(place_ref, *refs):
    own, out_ref = refs[:4], refs[4]
    for core in (0, 1):
        @pl.when(place_ref[1] == core)
        def _(core=core):
            for k in range(3):
                out_ref[k] = own[k + core][...]


def total_kernel(x_ref, *refs):
    out_ref = refs[-1]
    total = jnp.sum(x_ref[...].astype(jnp.float32), axis=0).astype(jnp.bfloat16)
    for i in range(out_ref.shape[0]):
        out_ref[i] = total


def stacked_queries(q_ref, first):
    return jnp.concatenate(
        [q_ref[pl.ds(first, QB), h * HD : (h + 1) * HD] for h in range(GROUP)], axis=0
    )


def lane_fold(op, x):
    out = x[:, :HD]
    for i in range(1, x.shape[1] // HD):
        out = op(out, x[:, i * HD : (i + 1) * HD])
    return out


def band_kernel(place_ref, listed_ref, q_ref, slash_ref, *refs):
    own, other = refs[:4], refs[4]
    (acc_ref, top_ref, sum_ref, token_ref), (diag, col, bias, kwin, vwin, s_scr) = refs[5:9], refs[9:]
    token_ref[...] = jnp.zeros_like(token_ref)
    rows = q_ref.shape[0]
    span = SLASH_MAX + QB
    lead = 7 * rows - rows - SLASH_MAX
    for i in range(7):
        piece = own[3 - i // 2] if i % 2 == 0 else other.at[2 - i // 2]
        kwin[i * rows : (i + 1) * rows] = piece[0]
        vwin[i * rows : (i + 1) * rows] = piece[1]

    at = SLASH_MAX - slash_ref[...]
    n_off = at.shape[1]
    major = lax.broadcasted_iota(jnp.int32, (32, n_off), 0) == at // HD
    minor = lax.broadcasted_iota(jnp.int32, (HD, n_off), 0) == at % HD
    hits = lax.dot_general(
        jnp.where(major, 1.0, 0.0).astype(jnp.bfloat16),
        jnp.where(minor, 1.0, 0.0).astype(jnp.bfloat16),
        NT,
        preferred_element_type=jnp.float32,
    )
    line = jnp.where(hits > 0.5, 0.0, MASKED)
    for i in range(span // HD):
        bias[:, i * HD : (i + 1) * HD] = jnp.broadcast_to(line[i : i + 1], (QB, HD))
    diag[...] = pltpu.roll(bias[...], 0, 1, stride=1, stride_axis=0)

    block = lax.broadcasted_iota(jnp.int32, (1, 7 * rows), 1) // BLK
    block = block + (place_ref[0] - 6) * (rows // BLK)
    out = block < 0
    for i in range(listed_ref.shape[1]):
        out = jnp.logical_or(out, block == listed_ref[0, i])
    col[...] = jnp.where(out, MASKED, 0.0)

    chunks = [(at, min(256, span - at)) for at in range(0, span, 256)]

    @pl.loop(0, rows // QB)
    def _(step):
        first = pl.multiple_of(step * QB, QB)
        base = pl.multiple_of(lead + step * QB, QB)
        bias[...] = diag[...] + col[:, pl.ds(base, span)]
        q = stacked_queries(q_ref, first)
        top = jnp.full((GROUP * QB, HD), MASKED, jnp.float32)
        for at, width in chunks:
            k = kwin[pl.ds(base + at, width), :]
            s = lax.dot_general(q, k, NT, preferred_element_type=jnp.float32)
            b = bias[:, at : at + width]
            s = s + jnp.concatenate([b] * GROUP, axis=0)
            s_scr[:, at : at + width] = s
            top = jnp.maximum(top, lane_fold(jnp.maximum, s))
        top = jnp.max(top, axis=1, keepdims=True)
        shift = top * SCALE
        acc = jnp.zeros((GROUP * QB, HD), jnp.float32)
        total = jnp.zeros((GROUP * QB, HD), jnp.float32)
        for at, width in chunks:
            p = jnp.exp2(s_scr[:, at : at + width] * SCALE - shift)
            total = total + lane_fold(jnp.add, p)
            v = vwin[pl.ds(base + at, width), :]
            acc = acc + jnp.dot(p.astype(jnp.bfloat16), v, preferred_element_type=jnp.float32)
        acc_ref[step] = acc
        sum_ref[step] = total
        top_ref[step] = jnp.broadcast_to(top, (GROUP * QB, HD))


def far_kernel(place_ref, listed_ref, q_ref, mine_ref, other_ref, acc_ref, top_ref, sum_ref,
               attended, kfar, vfar):
    rows = q_ref.shape[0]
    half = mine_ref.shape[0]
    flip = place_ref[1] * half
    for i in range(half):
        for j, ref in enumerate((mine_ref, other_ref)):
            at = (j * half + i) * BLK
            kfar[at : at + BLK] = ref[i, 0]
            vfar[at : at + BLK] = ref[i, 1]
    n_far = kfar.shape[0]
    chunks = [(at, 256) for at in range(0, n_far, 256)]
    lane = lax.broadcasted_iota(jnp.int32, (1, 256), 1)
    positions = []
    for at, width in chunks:
        pos = jnp.zeros((1, 256), jnp.int32)
        for i in range(width // BLK):
            slot = (at // BLK + i + flip) % (2 * half)
            pos = jnp.where(lane // BLK == i, listed_ref[0, slot], pos)
        positions.append(pos * BLK + lane % BLK)

    @pl.loop(0, rows // QB)
    def _(step):
        first = pl.multiple_of(step * QB, QB)
        q = stacked_queries(q_ref, first)
        q_pos = place_ref[0] * rows + first + lax.broadcasted_iota(jnp.int32, (QB, 256), 0)
        band_top = top_ref[step]
        top = band_top
        scores = []
        for (at, width), pos in zip(chunks, positions):
            s = lax.dot_general(q, kfar[at : at + width], NT, preferred_element_type=jnp.float32)
            b = jnp.where(pos <= q_pos, 0.0, MASKED)
            s = s + jnp.concatenate([b] * GROUP, axis=0)
            scores.append(s)
            top = jnp.maximum(top, lane_fold(jnp.maximum, s))
        top = jnp.max(top, axis=1, keepdims=True)
        shift = top * SCALE
        fade = jnp.exp2(band_top * SCALE - shift)
        acc = acc_ref[step] * fade
        total = sum_ref[step] * fade
        for (at, width), s in zip(chunks, scores):
            p = jnp.exp2(s * SCALE - shift)
            total = total + lane_fold(jnp.add, p)
            acc = acc + jnp.dot(
                p.astype(jnp.bfloat16), vfar[at : at + width], preferred_element_type=jnp.float32
            )
        out = (acc / jnp.sum(total, axis=1, keepdims=True)).astype(jnp.bfloat16)
        for h in range(GROUP):
            attended[pl.ds(first, QB), h * HD : (h + 1) * HD] = out[h * QB : (h + 1) * QB]


def project_kernel(att_ref, w_ref, out_ref, w_scr, sem_in, out_scr, sem_out):
    parts, span, inner = w_scr.shape
    width = 512

    def fetch(i):
        return pltpu.make_async_copy(w_ref.at[i * span : (i + 1) * span], w_scr.at[i], sem_in.at[i])

    def store(i):
        return pltpu.make_async_copy(
            out_scr.at[i], out_ref.at[:, i * span : (i + 1) * span], sem_out.at[i]
        )

    for i in range(parts):
        fetch(i).start()
    for i in range(parts):
        fetch(i).wait()
        for n in range(0, span, width):
            out_scr[i, :, n : n + width] = lax.dot_general(
                att_ref[...], w_scr[i, n : n + width], NT, preferred_element_type=jnp.float32
            ).astype(jnp.bfloat16)
        store(i).start()
    for i in range(parts):
        store(i).wait()


def after_kernel(x_ref, token_ref, out_ref):
    out_ref[...] = x_ref[...]


def after(x, token):
    return pl.pallas_call(
        after_kernel,
        in_specs=vmem(2),
        out_specs=vmem(1)[0],
        out_shape=jax.ShapeDtypeStruct(x.shape, x.dtype),
        name="after",
    )(x, token)


def swap(x):
    return lax.ppermute(x, "c", [(0, 1), (1, 0)])


def spread(x, axis):
    n = lax.axis_size(axis)
    return lax.all_to_all(jnp.broadcast_to(x[None], (n,) + x.shape), axis, 0, 0, tiled=True)


def summed(x):
    return jnp.sum(x.astype(jnp.float32), axis=0).astype(jnp.bfloat16)


def body(query, keys, values, vertical, slash, out_weight):
    rows, width = keys.shape
    n_ctx = lax.axis_size(CTX)
    n_y, n_zh = lax.axis_size("y"), lax.axis_size("zh")
    place = lax.axis_index(CTX)
    core = lax.axis_index("c")
    half = vertical.shape[1] // 2
    cols, inner = out_weight.shape[1], out_weight.shape[0]
    span = SLASH_MAX + QB
    bf16, f32 = jnp.bfloat16, jnp.float32
    smem = [pl.BlockSpec(memory_space=pltpu.SMEM)]
    hbm = [pl.BlockSpec(memory_space=pl.ANY)]
    where = jnp.stack([place, core]).astype(jnp.int32)

    def shape(*dims, dtype=bf16):
        return jax.ShapeDtypeStruct(dims, dtype)

    keep, send = pl.pallas_call(
        pick_kernel,
        in_specs=smem * 2 + vmem(2),
        out_specs=vmem(2),
        out_shape=[
            shape(half, 2, BLK, width),
            shape(half, 2, BLK, width),
        ],
        name="pick",
    )(where, vertical, keys, values)

    blocks, pair = pl.pallas_call(
        merge_kernel,
        in_specs=vmem(4),
        out_specs=vmem(2),
        out_shape=[
            shape(half, 2, BLK, width),
            shape(2, rows, width),
        ],
        name="merge",
    )(keep, swap(send), keys, values)

    w = lax.all_gather(out_weight.T, CTX, axis=0, tiled=True)

    def ahead(x, chips):
        return lax.ppermute(x, CTX, [(i, i + 2 * chips) for i in range(n_ctx - 2 * chips)])

    own = [pair] + [ahead(pair, chips) for chips in (1, 2, 3)]

    def total(x, copies, *before):
        return pl.pallas_call(
            total_kernel, in_specs=vmem(1) + hbm * len(before), out_specs=vmem(1)[0],
            out_shape=shape(copies, *x.shape[1:]), name="total",
        )(x, *before)

    blocks = blocks.reshape(n_zh * n_y, -1, width)
    parts = lax.all_to_all(blocks, ZY, 0, 0, tiled=True)
    parts = total(parts, n_zh * n_y)
    far_mine = lax.all_to_all(parts, ZY, 0, 0, tiled=True).reshape(half, 2, BLK, width)

    other = swap(pl.pallas_call(
        choose_kernel, in_specs=smem + vmem(4), out_specs=vmem(1)[0],
        out_shape=shape(3, 2, rows, width), name="choose",
    )(where, *own))

    steps = rows // QB
    stats = shape(steps, GROUP * QB, HD, dtype=f32)
    acc, top, sums, token = pl.pallas_call(
        band_kernel,
        in_specs=smem * 2 + vmem(7),
        out_specs=vmem(4),
        out_shape=[stats, stats, stats, shape(8, HD, dtype=f32)],
        scratch_shapes=[
            pltpu.VMEM((QB, span), f32),
            pltpu.VMEM((1, 7 * rows), f32),
            pltpu.VMEM((QB, span), f32),
            pltpu.VMEM((7 * rows, HD), bf16),
            pltpu.VMEM((7 * rows, HD), bf16),
            pltpu.VMEM((GROUP * QB, span), f32),
        ],
        compiler_params=pltpu.CompilerParams(vmem_limit_bytes=VMEM_LIMIT),
        cost_estimate=pl.CostEstimate(
            flops=8 * rows * GROUP * HD * span,
            bytes_accessed=8_000_000,
            transcendentals=rows * GROUP * span,
        ),
        name="band",
    )(where, vertical, query, slash, *own, other)

    far_other = swap(after(far_mine, token))
    n_far = 2 * half * BLK
    attended = pl.pallas_call(
        far_kernel,
        in_specs=smem * 2 + vmem(6),
        out_specs=vmem(1)[0],
        out_shape=shape(rows, GROUP * HD),
        scratch_shapes=[pltpu.VMEM((n_far, HD), bf16), pltpu.VMEM((n_far, HD), bf16)],
        compiler_params=pltpu.CompilerParams(vmem_limit_bytes=VMEM_LIMIT),
        cost_estimate=pl.CostEstimate(
            flops=8 * rows * GROUP * HD * n_far,
            bytes_accessed=8_000_000,
            transcendentals=rows * GROUP * n_far,
        ),
        name="far",
    )(where, vertical, query, far_mine, far_other, acc, top, sums)

    d_model = cols * n_ctx
    term = pl.pallas_call(
        project_kernel,
        in_specs=vmem(1) + hbm,
        out_specs=hbm[0],
        out_shape=shape(rows, d_model),
        scratch_shapes=[
            pltpu.VMEM((n_zh, d_model // n_zh, inner), bf16),
            pltpu.SemaphoreType.DMA((n_zh,)),
            pltpu.VMEM((n_zh, rows, d_model // n_zh), bf16),
            pltpu.SemaphoreType.DMA((n_zh,)),
        ],
        compiler_params=pltpu.CompilerParams(vmem_limit_bytes=VMEM_LIMIT),
        cost_estimate=pl.CostEstimate(
            flops=2 * rows * inner * d_model, bytes_accessed=8_000_000, transcendentals=0
        ),
        name="project",
    )(attended, w)
    n_kv = lax.axis_size(KV)
    received = lax.all_to_all(term.reshape(n_kv, rows // n_kv, d_model), KV, 0, 0, tiled=True)
    return summed(received)


def solution(mesh):
    fine = Mesh(mesh.devices.reshape(4, 8, 2, 4, 2), CTX + KV)
    return jax.shard_map(
        body,
        mesh=fine,
        in_specs=(
            P(CTX, KV),
            P(CTX, KV),
            P(CTX, KV),
            P(KV, None),
            P(KV, None),
            P(KV, CTX),
        ),
        out_specs=P(CTX + KV, None),
        check_vma=False,
    )
```

```python
import functools
import math

import jax
import jax.numpy as jnp
from jax import lax
from jax.experimental import pallas as pl
from jax.experimental.pallas import tpu as pltpu
from jax.sharding import Mesh, PartitionSpec as P

BLK = 64
SLASH_MAX = 2048
HD = 128
GROUP = 4
QB = 128
MASKED = -1e30
CTX = ("zh", "y", "c")
KV = ("x", "zl")
ZY = ("zh", "y")
SCALE = math.log2(math.e) / math.sqrt(HD)
NT = (((1,), (1,)), ((), ()))
MIB = 1024 * 1024
SMALL = pltpu.CompilerParams(vmem_limit_bytes=6 * MIB)


def vmem(n):
    return [pl.BlockSpec(memory_space=pltpu.VMEM)] * n


def pack_kernel(k_ref, v_ref, w_ref, pair_ref, pack_ref):
    rows, width = k_ref.shape
    pair_ref[0] = k_ref[...]
    pair_ref[1] = v_ref[...]
    pack_ref[:rows] = k_ref[...]
    pack_ref[rows : 2 * rows] = v_ref[...]
    cols = w_ref.shape[0]
    for i in range(w_ref.shape[1] // width):
        at = 2 * rows + i * cols
        pack_ref[at : at + cols] = w_ref[:, i * width : (i + 1) * width]


def pick_kernel(place_ref, listed_ref, pack_ref, ready_ref, out_ref, w_ref):
    n_dev, n_row, _ = pack_ref.shape
    rows = (n_row - w_ref.shape[1]) // 2
    per_shard = rows // BLK
    half = out_ref.shape[0]
    core = place_ref[1]
    for slot in range(half):
        block = listed_ref[0, slot + core * half]
        holder = lax.div(block, per_shard)
        here = lax.div(lax.rem(holder, place_ref[3]), 2) == place_ref[2]
        row = pl.multiple_of(lax.rem(block, per_shard) * BLK, BLK)
        dev = 2 * lax.div(holder, place_ref[3]) + lax.rem(holder, 2)
        for part in range(2):
            got = pack_ref[dev, pl.ds(part * rows + row, BLK), :].astype(jnp.float32)
            out_ref[slot, part] = jnp.where(here, got, 0.0).astype(jnp.bfloat16)
    for zh in range(n_dev // 2):
        w_ref[zh] = pack_ref[2 * zh + core, 2 * rows :]


def choose_kernel(place_ref, *refs):
    own, out_ref = refs[:4], refs[4]
    for core in (0, 1):
        @pl.when(place_ref[1] == core)
        def _(core=core):
            for k in range(3):
                out_ref[k] = own[k + core][...]


def total_kernel(x_ref, ready_ref, out_ref):
    total = jnp.sum(x_ref[...].astype(jnp.float32), axis=0).astype(jnp.bfloat16)
    for i in range(out_ref.shape[0]):
        out_ref[i] = total


def stacked_queries(q_ref, first):
    return jnp.concatenate(
        [q_ref[pl.ds(first, QB), h * HD : (h + 1) * HD] for h in range(GROUP)], axis=0
    )


def lane_fold(op, x):
    out = x[:, :HD]
    for i in range(1, x.shape[1] // HD):
        out = op(out, x[:, i * HD : (i + 1) * HD])
    return out


def band_kernel(place_ref, listed_ref, q_ref, slash_ref, *refs):
    own, other = refs[:4], refs[4]
    (acc_ref, top_ref, sum_ref, token_ref), (diag, col, bias, kwin, vwin, s_scr) = refs[5:9], refs[9:]
    token_ref[...] = jnp.zeros_like(token_ref)
    rows = q_ref.shape[0]
    span = SLASH_MAX + QB
    lead = 7 * rows - rows - SLASH_MAX
    for i in range(7):
        piece = own[3 - i // 2] if i % 2 == 0 else other.at[2 - i // 2]
        kwin[i * rows : (i + 1) * rows] = piece[0]
        vwin[i * rows : (i + 1) * rows] = piece[1]

    at = SLASH_MAX - slash_ref[...]
    n_off = at.shape[1]
    major = lax.broadcasted_iota(jnp.int32, (32, n_off), 0) == at // HD
    minor = lax.broadcasted_iota(jnp.int32, (HD, n_off), 0) == at % HD
    hits = lax.dot_general(
        jnp.where(major, 1.0, 0.0).astype(jnp.bfloat16),
        jnp.where(minor, 1.0, 0.0).astype(jnp.bfloat16),
        NT,
        preferred_element_type=jnp.float32,
    )
    line = jnp.where(hits > 0.5, 0.0, MASKED)
    for i in range(span // HD):
        bias[:, i * HD : (i + 1) * HD] = jnp.broadcast_to(line[i : i + 1], (QB, HD))
    diag[...] = pltpu.roll(bias[...], 0, 1, stride=1, stride_axis=0)

    block = lax.broadcasted_iota(jnp.int32, (1, 7 * rows), 1) // BLK
    block = block + (place_ref[0] - 6) * (rows // BLK)
    out = block < 0
    for i in range(listed_ref.shape[1]):
        out = jnp.logical_or(out, block == listed_ref[0, i])
    col[...] = jnp.where(out, MASKED, 0.0)

    chunks = [(at, min(256, span - at)) for at in range(0, span, 256)]

    @pl.loop(0, rows // QB)
    def _(step):
        first = pl.multiple_of(step * QB, QB)
        base = pl.multiple_of(lead + step * QB, QB)
        bias[...] = diag[...] + col[:, pl.ds(base, span)]
        q = stacked_queries(q_ref, first)
        top = jnp.full((GROUP * QB, HD), MASKED, jnp.float32)
        for at, width in chunks:
            k = kwin[pl.ds(base + at, width), :]
            s = lax.dot_general(q, k, NT, preferred_element_type=jnp.float32)
            b = bias[:, at : at + width]
            s = s + jnp.concatenate([b] * GROUP, axis=0)
            s_scr[:, at : at + width] = s
            top = jnp.maximum(top, lane_fold(jnp.maximum, s))
        top = jnp.max(top, axis=1, keepdims=True)
        shift = top * SCALE
        acc = jnp.zeros((GROUP * QB, HD), jnp.float32)
        total = jnp.zeros((GROUP * QB, HD), jnp.float32)
        for at, width in chunks:
            p = jnp.exp2(s_scr[:, at : at + width] * SCALE - shift)
            total = total + lane_fold(jnp.add, p)
            v = vwin[pl.ds(base + at, width), :]
            acc = acc + jnp.dot(p.astype(jnp.bfloat16), v, preferred_element_type=jnp.float32)
        acc_ref[step] = acc
        sum_ref[step] = total
        top_ref[step] = jnp.broadcast_to(top, (GROUP * QB, HD))


def far_kernel(place_ref, listed_ref, q_ref, mine_ref, other_ref, acc_ref, top_ref, sum_ref,
               attended, kfar, vfar):
    rows = q_ref.shape[0]
    half = mine_ref.shape[0]
    flip = place_ref[1] * half
    for i in range(half):
        for j, ref in enumerate((mine_ref, other_ref)):
            at = (j * half + i) * BLK
            kfar[at : at + BLK] = ref[i, 0]
            vfar[at : at + BLK] = ref[i, 1]
    n_far = kfar.shape[0]
    chunks = [(at, 256) for at in range(0, n_far, 256)]
    lane = lax.broadcasted_iota(jnp.int32, (1, 256), 1)
    positions = []
    for at, width in chunks:
        pos = jnp.zeros((1, 256), jnp.int32)
        for i in range(width // BLK):
            slot = (at // BLK + i + flip) % (2 * half)
            pos = jnp.where(lane // BLK == i, listed_ref[0, slot], pos)
        positions.append(pos * BLK + lane % BLK)

    @pl.loop(0, rows // QB)
    def _(step):
        first = pl.multiple_of(step * QB, QB)
        q = stacked_queries(q_ref, first)
        q_pos = place_ref[0] * rows + first + lax.broadcasted_iota(jnp.int32, (QB, 256), 0)
        band_top = top_ref[step]
        top = band_top
        scores = []
        for (at, width), pos in zip(chunks, positions):
            s = lax.dot_general(q, kfar[at : at + width], NT, preferred_element_type=jnp.float32)
            b = jnp.where(pos <= q_pos, 0.0, MASKED)
            s = s + jnp.concatenate([b] * GROUP, axis=0)
            scores.append(s)
            top = jnp.maximum(top, lane_fold(jnp.maximum, s))
        top = jnp.max(top, axis=1, keepdims=True)
        shift = top * SCALE
        fade = jnp.exp2(band_top * SCALE - shift)
        acc = acc_ref[step] * fade
        total = sum_ref[step] * fade
        for (at, width), s in zip(chunks, scores):
            p = jnp.exp2(s * SCALE - shift)
            total = total + lane_fold(jnp.add, p)
            acc = acc + jnp.dot(
                p.astype(jnp.bfloat16), vfar[at : at + width], preferred_element_type=jnp.float32
            )
        out = (acc / jnp.sum(total, axis=1, keepdims=True)).astype(jnp.bfloat16)
        for h in range(GROUP):
            attended[pl.ds(first, QB), h * HD : (h + 1) * HD] = out[h * QB : (h + 1) * QB]


def project_kernel(att_ref, w_ref, out_ref, w_scr, sem_in, out_scr, sem_out):
    n_y, n_core, n_zh, group, cols, width = w_ref.shape
    span = out_ref.shape[1] // n_zh
    step = 512
    per = step // (n_core * cols)

    def fetch(z, h):
        dst = w_scr.at[z, :, :, :, pl.ds(h * width, width)]
        return pltpu.make_async_copy(w_ref.at[:, :, z, h], dst, sem_in.at[z, h])

    def store(z):
        return pltpu.make_async_copy(
            out_scr.at[z], out_ref.at[:, z * span : (z + 1) * span], sem_out.at[z]
        )

    for z in range(n_zh):
        for h in range(group):
            fetch(z, h).start()
    for z in range(n_zh):
        for h in range(group):
            fetch(z, h).wait()
        for n in range(span // step):
            w = w_scr[z, n * per : (n + 1) * per].reshape(step, group * width)
            out_scr[z, :, n * step : (n + 1) * step] = lax.dot_general(
                att_ref[...], w, NT, preferred_element_type=jnp.float32
            ).astype(jnp.bfloat16)
        store(z).start()
    for z in range(n_zh):
        store(z).wait()


def swap(x):
    return lax.ppermute(x, "c", [(0, 1), (1, 0)])


def spread(x, axis):
    n = lax.axis_size(axis)
    return lax.all_to_all(jnp.broadcast_to(x[None], (n,) + x.shape), axis, 0, 0, tiled=True)


def summed(x):
    return jnp.sum(x.astype(jnp.float32), axis=0).astype(jnp.bfloat16)


def body(query, keys, values, vertical, slash, out_weight):
    rows, width = keys.shape
    n_ctx = lax.axis_size(CTX)
    n_y, n_zh = lax.axis_size("y"), lax.axis_size("zh")
    place = lax.axis_index(CTX)
    core = lax.axis_index("c")
    half = vertical.shape[1] // 2
    cols, inner = out_weight.shape[1], out_weight.shape[0]
    span = SLASH_MAX + QB
    bf16, f32 = jnp.bfloat16, jnp.float32
    smem = [pl.BlockSpec(memory_space=pltpu.SMEM)]
    hbm = [pl.BlockSpec(memory_space=pl.ANY)]
    per_zh = n_y * lax.axis_size("c")
    where = jnp.stack([place, core, lax.axis_index("y"), per_zh]).astype(jnp.int32)

    def shape(*dims, dtype=bf16):
        return jax.ShapeDtypeStruct(dims, dtype)

    pair, pack = pl.pallas_call(
        pack_kernel,
        in_specs=vmem(3),
        out_specs=vmem(2),
        out_shape=[shape(2, rows, width), shape(2 * rows + cols * GROUP, width)],
        compiler_params=SMALL,
        name="pack",
    )(keys, values, out_weight.T)
    pack = lax.all_gather(pack, ("zh", "c"), axis=0, tiled=False)

    own = [pair]
    for k in (1, 2, 3):
        own.append(lax.ppermute(pair, CTX, [(i, i + 2 * k) for i in range(n_ctx - 2 * k)]))
    other = swap(pl.pallas_call(
        choose_kernel, in_specs=smem + vmem(4), out_specs=vmem(1)[0],
        out_shape=shape(3, 2, rows, width), compiler_params=SMALL, name="choose",
    )(where, *own))

    blocks, wt = pl.pallas_call(
        pick_kernel,
        in_specs=smem * 2 + vmem(2),
        out_specs=vmem(2),
        out_shape=[
            shape(half, 2, BLK, width),
            shape(n_zh, cols * GROUP, width),
        ],
        compiler_params=SMALL,
        name="pick",
    )(where, vertical, pack, other)
    w = lax.all_gather(wt, ("y", "c"), axis=0, tiled=False)
    w = w.reshape(n_y, 2, n_zh, GROUP, cols, width)

    steps = rows // QB
    stats = shape(steps, GROUP * QB, HD, dtype=f32)
    acc, top, sums, token = pl.pallas_call(
        band_kernel,
        in_specs=smem * 2 + vmem(7),
        out_specs=vmem(4),
        out_shape=[stats, stats, stats, shape(8, HD, dtype=f32)],
        scratch_shapes=[
            pltpu.VMEM((QB, span), f32),
            pltpu.VMEM((1, 7 * rows), f32),
            pltpu.VMEM((QB, span), f32),
            pltpu.VMEM((7 * rows, HD), bf16),
            pltpu.VMEM((7 * rows, HD), bf16),
            pltpu.VMEM((GROUP * QB, span), f32),
        ],
        compiler_params=pltpu.CompilerParams(vmem_limit_bytes=20 * MIB),
        cost_estimate=pl.CostEstimate(
            flops=8 * rows * GROUP * HD * span,
            bytes_accessed=8_000_000,
            transcendentals=rows * GROUP * span,
        ),
        name="band",
    )(where, vertical, query, slash, *own, other)


    parts = lax.all_to_all(blocks, "y", 0, 0, tiled=True)
    parts = pl.pallas_call(
        total_kernel, in_specs=vmem(2), out_specs=vmem(1)[0],
        out_shape=shape(*parts.shape), compiler_params=SMALL, name="total",
    )(parts, token)
    far_mine = lax.all_to_all(parts, "y", 0, 0, tiled=True)
    far_other = swap(far_mine)
    n_far = 2 * half * BLK
    attended = pl.pallas_call(
        far_kernel,
        in_specs=smem * 2 + vmem(6),
        out_specs=vmem(1)[0],
        out_shape=shape(rows, GROUP * HD),
        scratch_shapes=[pltpu.VMEM((n_far, HD), bf16), pltpu.VMEM((n_far, HD), bf16)],
        compiler_params=pltpu.CompilerParams(vmem_limit_bytes=20 * MIB),
        cost_estimate=pl.CostEstimate(
            flops=8 * rows * GROUP * HD * n_far,
            bytes_accessed=8_000_000,
            transcendentals=rows * GROUP * n_far,
        ),
        name="far",
    )(where, vertical, query, far_mine, far_other, acc, top, sums)

    d_model = cols * n_ctx
    term = pl.pallas_call(
        project_kernel,
        in_specs=vmem(1) + hbm,
        out_specs=hbm[0],
        out_shape=shape(rows, d_model),
        scratch_shapes=[
            pltpu.VMEM((n_zh, n_y, 2, cols, inner), bf16),
            pltpu.SemaphoreType.DMA((n_zh, GROUP)),
            pltpu.VMEM((n_zh, rows, d_model // n_zh), bf16),
            pltpu.SemaphoreType.DMA((n_zh,)),
        ],
        compiler_params=pltpu.CompilerParams(vmem_limit_bytes=48 * MIB),
        cost_estimate=pl.CostEstimate(
            flops=2 * rows * inner * d_model, bytes_accessed=8_000_000, transcendentals=0
        ),
        name="project",
    )(attended, w)
    n_kv = lax.axis_size(KV)
    received = lax.all_to_all(term.reshape(n_kv, rows // n_kv, d_model), KV, 0, 0, tiled=True)
    return summed(received)


def solution(mesh):
    fine = Mesh(mesh.devices.reshape(4, 8, 2, 4, 2), CTX + KV)
    return jax.shard_map(
        body,
        mesh=fine,
        in_specs=(
            P(CTX, KV),
            P(CTX, KV),
            P(CTX, KV),
            P(KV, None),
            P(KV, None),
            P(KV, CTX),
        ),
        out_specs=P(CTX + KV, None),
        check_vma=False,
    )
```

```python
import functools
import math

import jax
import jax.numpy as jnp
from jax import lax
from jax.experimental import pallas as pl
from jax.experimental.pallas import tpu as pltpu
from jax.sharding import Mesh, PartitionSpec as P

BLK = 64
SLASH_MAX = 2048
HD = 128
GROUP = 4
QB = 128
MASKED = -1e30
CTX = ("zh", "y", "c")
KV = ("x", "zl")
ZY = ("zh", "y")
SCALE = math.log2(math.e) / math.sqrt(HD)
NT = (((1,), (1,)), ((), ()))
MIB = 1024 * 1024
SMALL = pltpu.CompilerParams(vmem_limit_bytes=6 * MIB)


def vmem(n):
    return [pl.BlockSpec(memory_space=pltpu.VMEM)] * n


def pack_kernel(k_ref, v_ref, w_ref, pair_ref, pack_ref):
    rows, width = k_ref.shape
    pair_ref[0] = k_ref[...]
    pair_ref[1] = v_ref[...]
    pack_ref[:rows] = k_ref[...]
    pack_ref[rows : 2 * rows] = v_ref[...]
    cols = w_ref.shape[0]
    for i in range(w_ref.shape[1] // width):
        at = 2 * rows + i * cols
        pack_ref[at : at + cols] = w_ref[:, i * width : (i + 1) * width]


def pick_kernel(place_ref, listed_ref, pack_ref, ready_ref, out_ref, w_ref):
    n_dev, n_row, _ = pack_ref.shape
    rows = (n_row - w_ref.shape[1]) // 2
    per_shard = rows // BLK
    half = out_ref.shape[0]
    core = place_ref[1]
    for slot in range(half):
        block = listed_ref[0, slot + core * half]
        holder = lax.div(block, per_shard)
        here = lax.div(lax.rem(holder, place_ref[3]), 2) == place_ref[2]
        row = pl.multiple_of(lax.rem(block, per_shard) * BLK, BLK)
        dev = 2 * lax.div(holder, place_ref[3]) + lax.rem(holder, 2)
        for part in range(2):
            got = pack_ref[dev, pl.ds(part * rows + row, BLK), :].astype(jnp.float32)
            out_ref[slot, part] = jnp.where(here, got, 0.0).astype(jnp.bfloat16)
    for zh in range(n_dev // 2):
        w_ref[zh] = pack_ref[2 * zh + core, 2 * rows :]


def choose_kernel(place_ref, *refs):
    own, out_ref = refs[:4], refs[4]
    for core in (0, 1):
        @pl.when(place_ref[1] == core)
        def _(core=core):
            for k in range(3):
                out_ref[k] = own[k + core][...]


def total_kernel(x_ref, ready_ref, out_ref):
    total = jnp.sum(x_ref[...].astype(jnp.float32), axis=0).astype(jnp.bfloat16)
    for i in range(out_ref.shape[0]):
        out_ref[i] = total


def stacked_queries(q_ref, first):
    return jnp.concatenate(
        [q_ref[pl.ds(first, QB), h * HD : (h + 1) * HD] for h in range(GROUP)], axis=0
    )


def lane_fold(op, x):
    out = x[:, :HD]
    for i in range(1, x.shape[1] // HD):
        out = op(out, x[:, i * HD : (i + 1) * HD])
    return out


def band_kernel(place_ref, listed_ref, q_ref, slash_ref, *refs):
    own, other = refs[:4], refs[4]
    (acc_ref, top_ref, sum_ref, token_ref), (diag, col, bias, kwin, vwin, s_scr) = refs[5:9], refs[9:]
    token_ref[...] = jnp.zeros_like(token_ref)
    rows = q_ref.shape[0]
    span = SLASH_MAX + QB
    lead = 7 * rows - rows - SLASH_MAX
    for i in range(7):
        piece = own[3 - i // 2] if i % 2 == 0 else other.at[2 - i // 2]
        kwin[i * rows : (i + 1) * rows] = piece[0]
        vwin[i * rows : (i + 1) * rows, :HD] = piece[1]
    vwin[:, HD:] = jnp.ones((7 * rows, HD), jnp.bfloat16)

    at = SLASH_MAX - slash_ref[...]
    n_off = at.shape[1]
    major = lax.broadcasted_iota(jnp.int32, (32, n_off), 0) == at // HD
    minor = lax.broadcasted_iota(jnp.int32, (HD, n_off), 0) == at % HD
    hits = lax.dot_general(
        jnp.where(major, 1.0, 0.0).astype(jnp.bfloat16),
        jnp.where(minor, 1.0, 0.0).astype(jnp.bfloat16),
        NT,
        preferred_element_type=jnp.float32,
    )
    line = jnp.where(hits > 0.5, 0.0, MASKED)
    for i in range(span // HD):
        bias[:, i * HD : (i + 1) * HD] = jnp.broadcast_to(line[i : i + 1], (QB, HD))
    diag[...] = pltpu.roll(bias[...], 0, 1, stride=1, stride_axis=0)

    block = lax.broadcasted_iota(jnp.int32, (1, 7 * rows), 1) // BLK
    block = block + (place_ref[0] - 6) * (rows // BLK)
    out = block < 0
    for i in range(listed_ref.shape[1]):
        out = jnp.logical_or(out, block == listed_ref[0, i])
    col[...] = jnp.where(out, MASKED, 0.0)

    chunks = [(at, min(256, span - at)) for at in range(0, span, 256)]

    @pl.loop(0, rows // QB)
    def _(step):
        first = pl.multiple_of(step * QB, QB)
        base = pl.multiple_of(lead + step * QB, QB)
        bias[...] = diag[...] + col[:, pl.ds(base, span)]
        q = stacked_queries(q_ref, first)
        top = jnp.full((GROUP * QB, HD), MASKED, jnp.float32)
        for at, width in chunks:
            k = kwin[pl.ds(base + at, width), :]
            s = lax.dot_general(q, k, NT, preferred_element_type=jnp.float32)
            b = bias[:, at : at + width]
            s = s + jnp.concatenate([b] * GROUP, axis=0)
            s_scr[:, at : at + width] = s
            top = jnp.maximum(top, lane_fold(jnp.maximum, s))
        top = jnp.max(top, axis=1, keepdims=True)
        shift = top * SCALE
        acc = jnp.zeros((GROUP * QB, 2 * HD), jnp.float32)
        for at, width in chunks:
            p = jnp.exp2(s_scr[:, at : at + width] * SCALE - shift)
            v = vwin[pl.ds(base + at, width), :]
            acc = acc + jnp.dot(p.astype(jnp.bfloat16), v, preferred_element_type=jnp.float32)
        acc_ref[step] = acc[:, :HD]
        sum_ref[step] = acc[:, HD:]
        top_ref[step] = jnp.broadcast_to(top, (GROUP * QB, HD))


def far_kernel(place_ref, listed_ref, q_ref, mine_ref, other_ref, acc_ref, top_ref, sum_ref,
               attended, kfar, vfar):
    rows = q_ref.shape[0]
    half = mine_ref.shape[0]
    flip = place_ref[1] * half
    for i in range(half):
        for j, ref in enumerate((mine_ref, other_ref)):
            at = (j * half + i) * BLK
            kfar[at : at + BLK] = ref[i, 0]
            vfar[at : at + BLK, :HD] = ref[i, 1]
    n_far = kfar.shape[0]
    vfar[:, HD:] = jnp.ones((n_far, HD), jnp.bfloat16)
    chunks = [(at, 256) for at in range(0, n_far, 256)]
    lane = lax.broadcasted_iota(jnp.int32, (1, 256), 1)
    positions = []
    for at, width in chunks:
        pos = jnp.zeros((1, 256), jnp.int32)
        for i in range(width // BLK):
            slot = (at // BLK + i + flip) % (2 * half)
            pos = jnp.where(lane // BLK == i, listed_ref[0, slot], pos)
        positions.append(pos * BLK + lane % BLK)

    @pl.loop(0, rows // QB)
    def _(step):
        first = pl.multiple_of(step * QB, QB)
        q = stacked_queries(q_ref, first)
        q_pos = place_ref[0] * rows + first + lax.broadcasted_iota(jnp.int32, (QB, 256), 0)
        band_top = top_ref[step]
        top = band_top
        scores = []
        for (at, width), pos in zip(chunks, positions):
            s = lax.dot_general(q, kfar[at : at + width], NT, preferred_element_type=jnp.float32)
            b = jnp.where(pos <= q_pos, 0.0, MASKED)
            s = s + jnp.concatenate([b] * GROUP, axis=0)
            scores.append(s)
            top = jnp.maximum(top, lane_fold(jnp.maximum, s))
        top = jnp.max(top, axis=1, keepdims=True)
        shift = top * SCALE
        fade = jnp.exp2(band_top * SCALE - shift)
        acc = jnp.zeros((GROUP * QB, 2 * HD), jnp.float32)
        for (at, width), s in zip(chunks, scores):
            p = jnp.exp2(s * SCALE - shift)
            acc = acc + jnp.dot(
                p.astype(jnp.bfloat16), vfar[at : at + width], preferred_element_type=jnp.float32
            )
        total = sum_ref[step] * fade + acc[:, HD:]
        out = ((acc_ref[step] * fade + acc[:, :HD]) / total).astype(jnp.bfloat16)
        for h in range(GROUP):
            attended[pl.ds(first, QB), h * HD : (h + 1) * HD] = out[h * QB : (h + 1) * QB]


def project_kernel(att_ref, w_ref, out_ref, w_scr, sem_in, out_scr, sem_out):
    n_y, n_core, n_zh, group, cols, width = w_ref.shape
    span = out_ref.shape[1] // n_zh
    step = 512
    per = step // (n_core * cols)

    def fetch(z, h):
        dst = w_scr.at[z, :, :, :, pl.ds(h * width, width)]
        return pltpu.make_async_copy(w_ref.at[:, :, z, h], dst, sem_in.at[z, h])

    def store(z):
        return pltpu.make_async_copy(
            out_scr.at[z], out_ref.at[:, z * span : (z + 1) * span], sem_out.at[z]
        )

    for z in range(n_zh):
        for h in range(group):
            fetch(z, h).start()
    for z in range(n_zh):
        for h in range(group):
            fetch(z, h).wait()
        for n in range(span // step):
            w = w_scr[z, n * per : (n + 1) * per].reshape(step, group * width)
            out_scr[z, :, n * step : (n + 1) * step] = lax.dot_general(
                att_ref[...], w, NT, preferred_element_type=jnp.float32
            ).astype(jnp.bfloat16)
        store(z).start()
    for z in range(n_zh):
        store(z).wait()


def swap(x):
    return lax.ppermute(x, "c", [(0, 1), (1, 0)])


def spread(x, axis):
    n = lax.axis_size(axis)
    return lax.all_to_all(jnp.broadcast_to(x[None], (n,) + x.shape), axis, 0, 0, tiled=True)


def summed(x):
    return jnp.sum(x.astype(jnp.float32), axis=0).astype(jnp.bfloat16)


def body(query, keys, values, vertical, slash, out_weight):
    rows, width = keys.shape
    n_ctx = lax.axis_size(CTX)
    n_y, n_zh = lax.axis_size("y"), lax.axis_size("zh")
    place = lax.axis_index(CTX)
    core = lax.axis_index("c")
    half = vertical.shape[1] // 2
    cols, inner = out_weight.shape[1], out_weight.shape[0]
    span = SLASH_MAX + QB
    bf16, f32 = jnp.bfloat16, jnp.float32
    smem = [pl.BlockSpec(memory_space=pltpu.SMEM)]
    hbm = [pl.BlockSpec(memory_space=pl.ANY)]
    per_zh = n_y * lax.axis_size("c")
    where = jnp.stack([place, core, lax.axis_index("y"), per_zh]).astype(jnp.int32)

    def shape(*dims, dtype=bf16):
        return jax.ShapeDtypeStruct(dims, dtype)

    pair, pack = pl.pallas_call(
        pack_kernel,
        in_specs=vmem(3),
        out_specs=vmem(2),
        out_shape=[shape(2, rows, width), shape(2 * rows + cols * GROUP, width)],
        compiler_params=SMALL,
        name="pack",
    )(keys, values, out_weight.T)
    pack = lax.all_gather(pack, ("zh", "c"), axis=0, tiled=False)

    own = [pair]
    for k in (1, 2, 3):
        own.append(lax.ppermute(pair, CTX, [(i, i + 2 * k) for i in range(n_ctx - 2 * k)]))
    other = swap(pl.pallas_call(
        choose_kernel, in_specs=smem + vmem(4), out_specs=vmem(1)[0],
        out_shape=shape(3, 2, rows, width), compiler_params=SMALL, name="choose",
    )(where, *own))

    blocks, wt = pl.pallas_call(
        pick_kernel,
        in_specs=smem * 2 + vmem(2),
        out_specs=vmem(2),
        out_shape=[
            shape(half, 2, BLK, width),
            shape(n_zh, cols * GROUP, width),
        ],
        compiler_params=SMALL,
        name="pick",
    )(where, vertical, pack, other)
    w = lax.all_gather(wt, ("y", "c"), axis=0, tiled=False)
    w = w.reshape(n_y, 2, n_zh, GROUP, cols, width)

    steps = rows // QB
    stats = shape(steps, GROUP * QB, HD, dtype=f32)
    acc, top, sums, token = pl.pallas_call(
        band_kernel,
        in_specs=smem * 2 + vmem(7),
        out_specs=vmem(4),
        out_shape=[stats, stats, stats, shape(8, HD, dtype=f32)],
        scratch_shapes=[
            pltpu.VMEM((QB, span), f32),
            pltpu.VMEM((1, 7 * rows), f32),
            pltpu.VMEM((QB, span), f32),
            pltpu.VMEM((7 * rows, HD), bf16),
            pltpu.VMEM((7 * rows, 2 * HD), bf16),
            pltpu.VMEM((GROUP * QB, span), f32),
        ],
        compiler_params=pltpu.CompilerParams(vmem_limit_bytes=20 * MIB),
        cost_estimate=pl.CostEstimate(
            flops=8 * rows * GROUP * HD * span,
            bytes_accessed=8_000_000,
            transcendentals=rows * GROUP * span,
        ),
        name="band",
    )(where, vertical, query, slash, *own, other)


    parts = lax.all_to_all(blocks, "y", 0, 0, tiled=True)
    parts = pl.pallas_call(
        total_kernel, in_specs=vmem(2), out_specs=vmem(1)[0],
        out_shape=shape(*parts.shape), compiler_params=SMALL, name="total",
    )(parts, token)
    far_mine = lax.all_to_all(parts, "y", 0, 0, tiled=True)
    far_other = swap(far_mine)
    n_far = 2 * half * BLK
    attended = pl.pallas_call(
        far_kernel,
        in_specs=smem * 2 + vmem(6),
        out_specs=vmem(1)[0],
        out_shape=shape(rows, GROUP * HD),
        scratch_shapes=[pltpu.VMEM((n_far, HD), bf16), pltpu.VMEM((n_far, 2 * HD), bf16)],
        compiler_params=pltpu.CompilerParams(vmem_limit_bytes=20 * MIB),
        cost_estimate=pl.CostEstimate(
            flops=8 * rows * GROUP * HD * n_far,
            bytes_accessed=8_000_000,
            transcendentals=rows * GROUP * n_far,
        ),
        name="far",
    )(where, vertical, query, far_mine, far_other, acc, top, sums)

    d_model = cols * n_ctx
    term = pl.pallas_call(
        project_kernel,
        in_specs=vmem(1) + hbm,
        out_specs=hbm[0],
        out_shape=shape(rows, d_model),
        scratch_shapes=[
            pltpu.VMEM((n_zh, n_y, 2, cols, inner), bf16),
            pltpu.SemaphoreType.DMA((n_zh, GROUP)),
            pltpu.VMEM((n_zh, rows, d_model // n_zh), bf16),
            pltpu.SemaphoreType.DMA((n_zh,)),
        ],
        compiler_params=pltpu.CompilerParams(vmem_limit_bytes=48 * MIB),
        cost_estimate=pl.CostEstimate(
            flops=2 * rows * inner * d_model, bytes_accessed=8_000_000, transcendentals=0
        ),
        name="project",
    )(attended, w)
    n_kv = lax.axis_size(KV)
    received = lax.all_to_all(term.reshape(n_kv, rows // n_kv, d_model), KV, 0, 0, tiled=True)
    return summed(received)


def solution(mesh):
    fine = Mesh(mesh.devices.reshape(4, 8, 2, 4, 2), CTX + KV)
    return jax.shard_map(
        body,
        mesh=fine,
        in_specs=(
            P(CTX, KV),
            P(CTX, KV),
            P(CTX, KV),
            P(KV, None),
            P(KV, None),
            P(KV, CTX),
        ),
        out_specs=P(CTX + KV, None),
        check_vma=False,
    )
```
